32 devices in a mesh: row: 16 (over z, y, x), col: 2 (over core).
Axes of the slice: x: 2, y: 2, z: 4, core: 2. Of those that a mesh axis runs over, the one named last changes fastest.
Arguments:
- panel: float32 [12288, 512], P(('row', 'col')), may hold values from -600 to 600
- trailing: float32 [12288, 1024], P('row', 'col'), may hold values from -6 to 6
Outputs:
- r_factor: float32 [512, 512], replicated
- residual: float32 [12288, 1024], P('row', 'col')
The draws below stay inside these ranges and needn't reach their ends.
All inputs are finite; a program needn't handle non-finite values.
Results may differ from the reference program's by a relative error of at most 0.0003.
Values sent between devices are 32-bit elements; how exact they have to be, the bound alone decides.
A program may use at most 64 MiB of HBM per device.

```python
import math
import jax
import jax.numpy as jnp
from jax import lax

B = 512
NROWS = 12288
NTRAIL = 1024


def draw_panel(key, part):
    keys = jax.random.split(key, 4)
    base = jax.random.normal(keys[0], (NROWS, B), jnp.float32)
    spread = 10.0
    mixing = jax.random.normal(keys[1], (B, B), jnp.float32) * (0.3 / math.sqrt(B))
    mixed = base + jnp.dot(base, mixing, precision=lax.Precision.HIGHEST)
    position = jnp.arange(NROWS, dtype=jnp.float32) / NROWS
    row_scale = jnp.exp(jax.random.uniform(keys[2], (NROWS,), jnp.float32, 0.0, math.log(spread))) * (1.0 + 2.0 * position)
    col_scale = jnp.exp(jax.random.uniform(keys[3], (B,), jnp.float32, 0.0, math.log(10.0)))
    return mixed * row_scale[:, None] * col_scale[None, :] * 0.1


def levels(stream_key, extent, cuts, least, largest):
    def one(dim, shards_of):
        steps = jax.random.uniform(jax.random.fold_in(jax.random.fold_in(stream_key, 6), dim), (shards_of,), jnp.float32, least / len(cuts), largest / len(cuts))
        return jnp.repeat(jnp.exp(steps), extent[dim] // shards_of).reshape((-1,) + (1,) * (len(extent) - dim - 1))

    loudness = one(*cuts[0])
    for cut in cuts[1:]:
        loudness = loudness * one(*cut)
    return loudness


def centred(own_key, dims, scale, most, shards=(), kind=jnp.bfloat16):
    gain = levels(own_key, dims, shards, -0.22, 0.18) if shards else 1.0
    values = jax.random.normal(own_key, dims, jnp.float32) * scale * gain
    return jnp.minimum(jnp.maximum(values, -most), most).astype(kind)


def setup_inputs(seed: int = 0) -> dict:
    arg_keys = jax.random.split(jax.random.key(seed), 3)
    panel = draw_panel(jax.random.fold_in(arg_keys[2], 71), 0)
    trailing = centred(arg_keys[1], (NROWS, NTRAIL), 1.0, 6.0, ((0, 16), (1, 2)), jnp.float32)
    return dict(panel=panel, trailing=trailing)


def reference(panel, trailing):
    basis, upper = jnp.linalg.qr(panel)
    signs = jnp.sign(jnp.diagonal(upper))
    upper = upper * signs[:, None]
    basis = basis * signs[None, :]
    coupling = jnp.dot(basis.T.astype(jnp.float32), trailing.astype(jnp.float32), precision=lax.Precision.HIGHEST, preferred_element_type=jnp.float32)
    residual = trailing - jnp.dot(basis.astype(jnp.float32), coupling.astype(jnp.float32), precision=lax.Precision.HIGHEST, preferred_element_type=jnp.float32)
    r_factor = upper / jnp.sqrt(jnp.float32(NROWS))
    return (r_factor, residual)
```

```python
import functools, math
import jax
import jax.numpy as jnp
from jax import lax
from jax.experimental import pallas as pl
from jax.experimental.pallas import tpu as pltpu
from jax.sharding import PartitionSpec as P

HI = lax.Precision.HIGHEST
NB = 128
G = 16
TN = (((0,), (0,)), ((), ()))


def split3(x):
    h = x.astype(jnp.bfloat16).astype(jnp.float32)
    rest = x - h
    m = rest.astype(jnp.bfloat16).astype(jnp.float32)
    return h, m, rest - m


def factor_block(d_ref):
    rows = lax.broadcasted_iota(jnp.int32, (G, NB), 0)
    for r0 in range(0, NB, G):
        left, right = d_ref[r0:r0 + G, :NB], d_ref[r0:r0 + G, NB:]
        cols = [jnp.broadcast_to(left[:, r0 + j:r0 + j + 1], (G, NB)) for j in range(G)]
        scale = jnp.zeros((G, NB), jnp.float32)
        for j in range(G):
            pivot = jnp.broadcast_to(cols[j][j:j + 1], (G, NB))
            inv = 1.0 / pivot
            scale = jnp.where(rows == j, lax.rsqrt(pivot), scale)
            below = jnp.where(rows > j, cols[j] * inv, 0.0)
            for c in range(j + 1, G):
                cols[c] = cols[c] - below * cols[c][j:j + 1]
            left = left - below * left[j:j + 1]
            right = right - below * right[j:j + 1]
        left, right = left * scale, right * scale
        d_ref[r0:r0 + G, :NB] = left
        d_ref[r0:r0 + G, NB:] = right
        if r0 + G < NB:
            both = jnp.concatenate([left, right], axis=1)
            h, m, l = split3(both)
            a = jnp.concatenate([v[:, :NB] for v in (h, h, m, m, h, l)], axis=0)
            b = jnp.concatenate([h, m, h, m, l, h], axis=0).astype(jnp.bfloat16)
            at = a.T.astype(jnp.bfloat16)
            upd = jnp.dot(at, b, preferred_element_type=jnp.float32)
            d_ref[r0 + G:, :] = d_ref[r0 + G:, :] - upd[r0 + G:, :]


def factor(m_ref, d_ref, size, between):
    eye = (lax.broadcasted_iota(jnp.int32, (NB, NB), 0) == lax.broadcasted_iota(jnp.int32, (NB, NB), 1)).astype(jnp.float32)
    steps = size // NB

    def step(k, _):
        at = pl.ds(pl.multiple_of(k * NB, NB), NB)
        d_ref[:, :NB] = m_ref[at, at]
        d_ref[:, NB:] = eye
        factor_block(d_ref)
        m_ref[at, :] = jnp.dot(d_ref[:, NB:], m_ref[at, :], precision=HI, preferred_element_type=jnp.float32)

        def below(i, _):
            to = pl.ds(pl.multiple_of(i * NB, NB), NB)
            m_ref[to, :] = m_ref[to, :] - lax.dot_general(m_ref[at, to], m_ref[at, :], TN, precision=HI, preferred_element_type=jnp.float32)
            return 0

        lax.fori_loop(k + 1, steps, below, 0)
        between(k)
        return 0

    lax.fori_loop(0, steps, step, 0)


class Sum:
    def __init__(self, n1, n2, part, got1, mid, got2, full, send, recv):
        self.n1, self.n2 = n1, n2
        self.part, self.got1, self.mid, self.got2, self.full = part, got1, mid, got2, full
        self.send, self.recv = send, recv
        me = lax.axis_index("row")
        self.outer, self.inner = me // n1, lax.rem(me, n1)
        self.col = lax.axis_index("col")

    def copies(self, phase):
        n1, n2, inner, outer = self.n1, self.n2, self.inner, self.outer
        first = (0, n1 - 1, n1 + n2 - 2, n1 + 2 * n2 - 3)[phase]
        out = []
        for k in range(1, n1 if phase in (0, 3) else n2):
            if phase in (0, 3):
                peer = lax.rem(inner + k, n1)
                target = outer * n1 + peer
            else:
                peer = lax.rem(outer + k, n2)
                target = peer * n1 + inner
            if phase == 0:
                src, dst = self.part.at[peer], self.got1.at[k - 1]
            elif phase == 1:
                src, dst = self.mid.at[peer], self.got2.at[k - 1]
            elif phase == 2:
                src = dst = self.full.at[inner, outer]
            else:
                src = dst = self.full.at[inner]
            out.append(pltpu.make_async_remote_copy(
                src_ref=src, dst_ref=dst, send_sem=self.send.at[first + k - 1],
                recv_sem=self.recv.at[first + k - 1], device_id=(target, self.col),
                device_id_type=pl.DeviceIdType.MESH))
        return out

    def start(self, phase):
        for copy in self.copies(phase):
            copy.start()

    def finish(self, phase):
        if phase == 0:
            total = self.part[self.inner]
            for k, copy in enumerate(self.copies(0)):
                copy.wait_recv()
                total = total + self.got1[k]
            self.mid[...] = total
        elif phase == 1:
            total = self.mid[self.outer]
            for k, copy in enumerate(self.copies(1)):
                copy.wait_recv()
                total = total + self.got2[k]
            self.full[self.inner, self.outer] = total
        else:
            for copy in self.copies(phase):
                copy.wait_recv()

    def drain(self):
        for phase in range(4):
            for copy in self.copies(phase):
                copy.wait_send()


def kernel(n, m, n1, split, total_rows, panel_ref, trailing_ref, r_ref, out_ref, block, gpart, ggot1, gmid, ggot2, gfull,
           cpart, cgot1, cmid, cgot2, cfull, m_ref, d_ref, gsend, grecv, csend, crecv, bsend, brecv, esend, erecv):
    n2 = n // n1
    size = panel_ref.shape[1]
    own = panel_ref.shape[0]
    row, col = lax.axis_index("row"), lax.axis_index("col")
    outer, inner = row // n1, lax.rem(row, n1)
    MESH = pl.DeviceIdType.MESH
    barrier = pltpu.get_barrier_semaphore()
    for k in range(1, m):
        pl.semaphore_signal(barrier, inc=1, device_id=(row, lax.rem(col + k, m)), device_id_type=MESH)
    for k in range(1, n1):
        pl.semaphore_signal(barrier, inc=1, device_id=(outer * n1 + lax.rem(inner + k, n1), col), device_id_type=MESH)
    for k in range(1, n2):
        pl.semaphore_signal(barrier, inc=1, device_id=(lax.rem(outer + k, n2) * n1 + inner, col), device_id_type=MESH)
    pl.semaphore_wait(barrier, m + n1 + n2 - 3)

    def spread(src, dst, send, recv):
        return [pltpu.make_async_remote_copy(
            src_ref=src, dst_ref=dst, send_sem=send.at[k - 1], recv_sem=recv.at[k - 1],
            device_id=(row, lax.rem(col + k, m)), device_id_type=MESH) for k in range(1, m)]

    gather = spread(panel_ref, block.at[col], bsend, brecv)
    for copy in gather:
        copy.start()
    block[col] = panel_ref[...]

    def tn(a, b):
        return lax.dot_general(a, b, TN, precision=HI, preferred_element_type=jnp.float32)

    half = size // split
    cols = pl.ds(pl.multiple_of(col * half, half), half) if split > 1 else pl.ds(0, size)
    total = tn(panel_ref[:, cols], panel_ref[...])
    for k, copy in enumerate(gather):
        copy.wait_recv()
        other = lax.rem(col + m - k - 1, m)
        total = total + tn(block[other, :, cols], block[other])
    gpart[...] = total.reshape(gpart.shape)
    gsum = Sum(n1, n2, gpart, ggot1, gmid, ggot2, gfull.at[col if split > 1 else 0], gsend, grecv)
    csum = Sum(n1, n2, cpart, cgot1, cmid, cgot2, cfull, csend, crecv)
    gsum.start(0)
    cross = tn(block[0], trailing_ref[:own, :])
    for k in range(1, m):
        cross = cross + tn(block[k], trailing_ref[k * own:(k + 1) * own, :])
    cpart[...] = cross.reshape(cpart.shape)
    for phase in range(4):
        gsum.finish(phase)
        if phase < 3:
            gsum.start(phase + 1)
    share = spread(gsum.full, gsum.full, esend, erecv) if split > 1 else []
    for copy in share:
        copy.start()
    csum.start(0)
    for copy in share:
        copy.wait_recv()
    m_ref[:, :size] = gfull[...].reshape(size, size)
    r = lax.broadcasted_iota(jnp.int32, (size, size), 0)
    c = lax.broadcasted_iota(jnp.int32, (size, size), 1)
    m_ref[:, size:] = (r == c).astype(jnp.float32)

    steps = size // NB

    def between(k):
        for phase in range(4):
            @pl.when(k == phase * (steps - 1) // 3)
            def _():
                csum.finish(phase)
                if phase < 3:
                    csum.start(phase + 1)

    factor(m_ref, d_ref, size, between)
    r = lax.broadcasted_iota(jnp.int32, (size, size), 0)
    c = lax.broadcasted_iota(jnp.int32, (size, size), 1)
    r_ref[...] = jnp.where(c >= r, m_ref[:, :size] * (1.0 / math.sqrt(total_rows)), 0.0)
    w = m_ref[:, size:]
    coupling = jnp.dot(w, cfull[...].reshape(size, cfull.shape[-1]), precision=HI, preferred_element_type=jnp.float32)
    combined = tn(w, coupling)
    for k in range(m):
        at = slice(k * own, (k + 1) * own)
        out_ref[at, :] = trailing_ref[at, :] - jnp.dot(block[k], combined, precision=HI, preferred_element_type=jnp.float32)
    gsum.drain()
    csum.drain()
    for copy in gather + share:
        copy.wait_send()


def per_device(panel, trailing):
    n, m = lax.axis_size("row"), lax.axis_size("col")
    own, size = panel.shape
    width = trailing.shape[1]
    n1 = 4 if n % 4 == 0 else n
    n2 = n // n1
    split = m if size % (8 * n * m) == 0 and (size // m) % 128 == 0 else 1
    f32 = jnp.float32

    def buffers(rows, cols, copies):
        s = rows // n
        lead = (copies,) if copies else ()
        return [pltpu.VMEM((n1, n2, s, cols), f32), pltpu.VMEM((max(n1 - 1, 1), n2, s, cols), f32),
                pltpu.VMEM((n2, s, cols), f32), pltpu.VMEM((max(n2 - 1, 1), s, cols), f32),
                pltpu.VMEM(lead + (n1, n2, s, cols), f32)]

    dma = pltpu.SemaphoreType.DMA
    hops = 2 * (n1 + n2 - 2)
    vmem = pl.BlockSpec(memory_space=pltpu.VMEM)
    return pl.pallas_call(
        functools.partial(kernel, n, m, n1, split, own * n * m),
        out_shape=(jax.ShapeDtypeStruct((size, size), f32), jax.ShapeDtypeStruct(trailing.shape, f32)),
        in_specs=[vmem] * 2,
        out_specs=[vmem] * 2,
        scratch_shapes=[pltpu.VMEM((m, own, size), f32)] + buffers(size // split, size, split) + buffers(size, width, 0)
        + [pltpu.VMEM((size, 2 * size), f32), pltpu.VMEM((NB, 2 * NB), f32)]
        + [dma((hops,))] * 4 + [dma((max(m - 1, 1),))] * 4,
        compiler_params=pltpu.CompilerParams(collective_id=0, has_side_effects=True, vmem_limit_bytes=56 << 20),
    )(panel, trailing)


def solution(mesh):
    return jax.shard_map(
        per_device, mesh=mesh, in_specs=(P(("row", "col"), None), P("row", "col")),
        out_specs=(P(), P("row", "col")), check_vma=False)
```

```python
import functools, math
import jax
import jax.numpy as jnp
from jax import lax
from jax.experimental import pallas as pl
from jax.experimental.pallas import tpu as pltpu
from jax.sharding import PartitionSpec as P

NB = 128
G = 16
TN = (((0,), (0,)), ((), ()))


NN = (((1,), (0,)), ((), ()))


def split2(x):
    h = x.astype(jnp.bfloat16)
    return h, (x - h.astype(jnp.float32)).astype(jnp.bfloat16)


def dot3(a, b, dims=NN):
    def dot(x, y):
        return lax.dot_general(x, y, dims, preferred_element_type=jnp.float32)
    return dot(a[0], b[0]) + (dot(a[0], b[1]) + dot(a[1], b[0]))


def split3(x):
    h = x.astype(jnp.bfloat16).astype(jnp.float32)
    rest = x - h
    m = rest.astype(jnp.bfloat16).astype(jnp.float32)
    return h, m, rest - m


def factor_block(d_ref):
    rows = lax.broadcasted_iota(jnp.int32, (G, NB), 0)
    for r0 in range(0, NB, G):
        left, right = d_ref[r0:r0 + G, :NB], d_ref[r0:r0 + G, NB:]
        cols = [jnp.broadcast_to(left[:, r0 + j:r0 + j + 1], (G, NB)) for j in range(G)]
        scale = jnp.zeros((G, NB), jnp.float32)
        for j in range(G):
            pivot = jnp.broadcast_to(cols[j][j:j + 1], (G, NB))
            inv = 1.0 / pivot
            scale = jnp.where(rows == j, lax.rsqrt(pivot), scale)
            below = jnp.where(rows > j, cols[j] * inv, 0.0)
            for c in range(j + 1, G):
                cols[c] = cols[c] - below * cols[c][j:j + 1]
            left = left - below * left[j:j + 1]
            right = right - below * right[j:j + 1]
        left, right = left * scale, right * scale
        d_ref[r0:r0 + G, :NB] = left
        d_ref[r0:r0 + G, NB:] = right
        if r0 + G < NB:
            both = jnp.concatenate([left, right], axis=1)
            h, m, l = split3(both)
            a = jnp.concatenate([v[:, :NB] for v in (h, h, m, m, h, l)], axis=0)
            b = jnp.concatenate([h, m, h, m, l, h], axis=0).astype(jnp.bfloat16)
            at = a.T.astype(jnp.bfloat16)
            upd = jnp.dot(at, b, preferred_element_type=jnp.float32)
            d_ref[r0 + G:, :] = d_ref[r0 + G:, :] - upd[r0 + G:, :]


def factor(m_ref, d_ref, size, between):
    eye = (lax.broadcasted_iota(jnp.int32, (NB, NB), 0) == lax.broadcasted_iota(jnp.int32, (NB, NB), 1)).astype(jnp.float32)
    steps = size // NB
    for k in range(steps):
        at, window = slice(k * NB, (k + 1) * NB), slice(k * NB, (k + 1) * NB + size)
        d_ref[:, :NB] = m_ref[at, at]
        d_ref[:, NB:] = eye
        factor_block(d_ref)
        done = dot3(split2(d_ref[:, NB:]), split2(m_ref[at, window]))
        m_ref[at, window] = done
        if k + 1 < steps:
            done = split2(done)
            right = tuple(v[:, NB:size - k * NB] for v in done)
            m_ref[(k + 1) * NB:, window] = m_ref[(k + 1) * NB:, window] - dot3(right, done, TN)
        between(k + 1)


def tiles(steps, split, col):
    if split == 1:
        return [(i, j) for i in range(steps) for j in range(i, steps)]
    first = [(col, col + t) for t in range(steps - col)]
    return first + [(steps - 1 - col, j) for j in range(steps - 1 - col, steps)]


class Sum:
    def __init__(self, n1, n2, part, got1, mid, got2, full, send, recv):
        self.n1, self.n2 = n1, n2
        self.part, self.got1, self.mid, self.got2, self.full = part, got1, mid, got2, full
        self.send, self.recv = send, recv
        me = lax.axis_index("row")
        self.outer, self.inner = me // n1, lax.rem(me, n1)
        self.col = lax.axis_index("col")

    def copies(self, phase):
        n1, n2, inner, outer = self.n1, self.n2, self.inner, self.outer
        first = (0, n1 - 1, n1 + n2 - 2, n1 + 2 * n2 - 3)[phase]
        out = []
        for k in range(1, n1 if phase in (0, 3) else n2):
            if phase in (0, 3):
                peer = lax.rem(inner + k, n1)
                target = outer * n1 + peer
            else:
                peer = lax.rem(outer + k, n2)
                target = peer * n1 + inner
            if phase == 0:
                src, dst = self.part.at[peer], self.got1.at[k - 1]
            elif phase == 1:
                src, dst = self.mid.at[peer], self.got2.at[k - 1]
            elif phase == 2:
                src = dst = self.full.at[inner, outer]
            else:
                src = dst = self.full.at[inner]
            out.append(pltpu.make_async_remote_copy(
                src_ref=src, dst_ref=dst, send_sem=self.send.at[first + k - 1],
                recv_sem=self.recv.at[first + k - 1], device_id=(target, self.col),
                device_id_type=pl.DeviceIdType.MESH))
        return out

    def start(self, phase):
        for copy in self.copies(phase):
            copy.start()

    def finish(self, phase):
        if phase == 0:
            total = self.part[self.inner]
            for k, copy in enumerate(self.copies(0)):
                copy.wait_recv()
                total = total + self.got1[k]
            self.mid[...] = total
        elif phase == 1:
            total = self.mid[self.outer]
            for k, copy in enumerate(self.copies(1)):
                copy.wait_recv()
                total = total + self.got2[k]
            self.full[self.inner, self.outer] = total
        else:
            for copy in self.copies(phase):
                copy.wait_recv()

    def drain(self):
        for phase in range(4):
            for copy in self.copies(phase):
                copy.wait_send()


def kernel(n, m, n1, split, total_rows, panel_ref, trailing_ref, r_ref, out_ref, block, strip, gpart, ggot1, gmid, ggot2, gfull,
           cpart, cgot1, cmid, cgot2, cfull, m_ref, d_ref, gsend, grecv, csend, crecv, bsend, brecv, esend, erecv):
    n2 = n // n1
    size = panel_ref.shape[1]
    own = panel_ref.shape[0]
    row, col = lax.axis_index("row"), lax.axis_index("col")
    outer, inner = row // n1, lax.rem(row, n1)
    MESH = pl.DeviceIdType.MESH
    barrier = pltpu.get_barrier_semaphore()
    for k in range(1, m):
        pl.semaphore_signal(barrier, inc=1, device_id=(row, lax.rem(col + k, m)), device_id_type=MESH)
    for k in range(1, n1):
        pl.semaphore_signal(barrier, inc=1, device_id=(outer * n1 + lax.rem(inner + k, n1), col), device_id_type=MESH)
    for k in range(1, n2):
        pl.semaphore_signal(barrier, inc=1, device_id=(lax.rem(outer + k, n2) * n1 + inner, col), device_id_type=MESH)
    pl.semaphore_wait(barrier, m + n1 + n2 - 3)

    def spread(src, dst, send, recv):
        return [pltpu.make_async_remote_copy(
            src_ref=src, dst_ref=dst, send_sem=send.at[k - 1], recv_sem=recv.at[k - 1],
            device_id=(row, lax.rem(col + k, m)), device_id_type=MESH) for k in range(1, m)]

    gather = spread(panel_ref, block.at[col], bsend, brecv)
    for copy in gather:
        copy.start()
    block[col] = panel_ref[...]

    steps = size // NB
    count = len(tiles(steps, split, 0))
    m_ref[:, :size] = jnp.zeros((size, size), jnp.float32)
    r = lax.broadcasted_iota(jnp.int32, (size, size), 0)
    c = lax.broadcasted_iota(jnp.int32, (size, size), 1)
    m_ref[:, size:] = (r == c).astype(jnp.float32)

    def cut(x, i):
        return x[:, pl.ds(pl.multiple_of(i * NB, NB), NB)]

    strips = range(steps) if split == 1 else (col, steps - 1 - col)

    def gram(x):
        return dot3(split2(jnp.concatenate([cut(x, i) for i in strips], axis=1)), split2(x[...]), TN)

    strip[...] = gram(panel_ref)
    for k, copy in enumerate(gather):
        copy.wait_recv()
        strip[...] = strip[...] + gram(block.at[lax.rem(col + m - k - 1, m)])
    if split == 1:
        picked = [strip[i * NB:(i + 1) * NB, j * NB:(j + 1) * NB] for i, j in tiles(steps, 1, 0)]
    else:
        picked = []
        for t in range(count):
            low = t >= steps - col
            i, j = jnp.where(low, 1, 0), jnp.where(low, t - 1, col + t)
            picked.append(strip[pl.ds(pl.multiple_of(i * NB, NB), NB), pl.ds(pl.multiple_of(j * NB, NB), NB)])
    gpart[...] = jnp.concatenate(picked, axis=0).reshape(gpart.shape)
    gsum = Sum(n1, n2, gpart, ggot1, gmid, ggot2, gfull.at[col if split > 1 else 0], gsend, grecv)
    csum = Sum(n1, n2, cpart, cgot1, cmid, cgot2, cfull, csend, crecv)
    gsum.start(0)
    cross = jnp.zeros((size, trailing_ref.shape[1]), jnp.float32)
    for k in range(m):
        cross = cross + dot3(split2(block[k]), split2(trailing_ref[k * own:(k + 1) * own, :]), TN)
    cpart[...] = cross.reshape(cpart.shape)
    for phase in range(4):
        gsum.finish(phase)
        if phase < 3:
            gsum.start(phase + 1)
        if phase == 0:
            csum.start(0)
    share = spread(gsum.full, gsum.full, esend, erecv) if split > 1 else []
    for copy in share:
        copy.start()
    for copy in share:
        copy.wait_recv()
    for k in range(split):
        flat = gfull[k].reshape(count * NB, NB)
        for t, (i, j) in enumerate(tiles(steps, split, k)):
            m_ref[i * NB:(i + 1) * NB, j * NB:(j + 1) * NB] = flat[t * NB:(t + 1) * NB]

    def between(k):
        for phase in range(4):
            if k == (steps if phase == 3 else phase * steps // 4):
                csum.finish(phase)
                if phase < 3:
                    csum.start(phase + 1)

    between(0)
    factor(m_ref, d_ref, size, between)
    r_ref[...] = jnp.where(c >= r, m_ref[:, :size] * (1.0 / math.sqrt(total_rows)), 0.0)
    w = split2(m_ref[:, size:])
    coupling = dot3(w, split2(cfull[...].reshape(size, cfull.shape[-1])))
    combined = split2(dot3(w, split2(coupling), TN))
    for k in range(m):
        at = slice(k * own, (k + 1) * own)
        out_ref[at, :] = trailing_ref[at, :] - dot3(split2(block[k]), combined)
    gsum.drain()
    csum.drain()
    for copy in gather + share:
        copy.wait_send()


def per_device(panel, trailing):
    n, m = lax.axis_size("row"), lax.axis_size("col")
    own, size = panel.shape
    width = trailing.shape[1]
    n1 = 4 if n % 4 == 0 else n
    n2 = n // n1
    steps = size // NB
    split = m if steps == 2 * m and (steps + 1) * NB % (8 * n) == 0 else 1
    count = len(tiles(steps, split, 0))
    f32 = jnp.float32

    def buffers(rows, cols, copies):
        s = rows // n
        lead = (copies,) if copies else ()
        return [pltpu.VMEM((n1, n2, s, cols), f32), pltpu.VMEM((max(n1 - 1, 1), n2, s, cols), f32),
                pltpu.VMEM((n2, s, cols), f32), pltpu.VMEM((max(n2 - 1, 1), s, cols), f32),
                pltpu.VMEM(lead + (n1, n2, s, cols), f32)]

    dma = pltpu.SemaphoreType.DMA
    hops = 2 * (n1 + n2 - 2)
    vmem = pl.BlockSpec(memory_space=pltpu.VMEM)
    return pl.pallas_call(
        functools.partial(kernel, n, m, n1, split, own * n * m),
        out_shape=(jax.ShapeDtypeStruct((size, size), f32), jax.ShapeDtypeStruct(trailing.shape, f32)),
        in_specs=[vmem] * 2,
        out_specs=[vmem] * 2,
        scratch_shapes=[pltpu.VMEM((m, own, size), f32), pltpu.VMEM((size if split == 1 else 2 * NB, size), f32)]
        + buffers(count * NB, NB, split) + buffers(size, width, 0)
        + [pltpu.VMEM((size, 2 * size), f32), pltpu.VMEM((NB, 2 * NB), f32)]
        + [dma((hops,))] * 4 + [dma((max(m - 1, 1),))] * 4,
        compiler_params=pltpu.CompilerParams(collective_id=0, has_side_effects=True, vmem_limit_bytes=56 << 20),
    )(panel, trailing)


def solution(mesh):
    return jax.shard_map(
        per_device, mesh=mesh, in_specs=(P(("row", "col"), None), P("row", "col")),
        out_specs=(P(), P("row", "col")), check_vma=False)
```

```python
import functools, math
import jax
import jax.numpy as jnp
from jax import lax
from jax.experimental import pallas as pl
from jax.experimental.pallas import tpu as pltpu
from jax.sharding import PartitionSpec as P

NB = 128
G = 16
TN = (((0,), (0,)), ((), ()))


NN = (((1,), (0,)), ((), ()))


def split2(x):
    h = x.astype(jnp.bfloat16)
    return h, (x - h.astype(jnp.float32)).astype(jnp.bfloat16)


def dot3(a, b, dims=NN):
    def dot(x, y):
        return lax.dot_general(x, y, dims, preferred_element_type=jnp.float32)
    return dot(a[0], b[0]) + (dot(a[0], b[1]) + dot(a[1], b[0]))


def split3(x):
    h = x.astype(jnp.bfloat16).astype(jnp.float32)
    rest = x - h
    m = rest.astype(jnp.bfloat16).astype(jnp.float32)
    return h, m, rest - m


def factor_block(d_ref):
    rows = lax.broadcasted_iota(jnp.int32, (G, NB), 0)
    for r0 in range(0, NB, G):
        left, right = d_ref[r0:r0 + G, :NB], d_ref[r0:r0 + G, NB:]
        cols = [jnp.broadcast_to(left[:, r0 + j:r0 + j + 1], (G, NB)) for j in range(G)]
        scale = jnp.zeros((G, NB), jnp.float32)
        for j in range(G):
            pivot = jnp.broadcast_to(cols[j][j:j + 1], (G, NB))
            inv = 1.0 / pivot
            scale = jnp.where(rows == j, lax.rsqrt(pivot), scale)
            below = jnp.where(rows > j, cols[j] * inv, 0.0)
            for c in range(j + 1, G):
                cols[c] = cols[c] - below * cols[c][j:j + 1]
            left = left - below * left[j:j + 1]
            right = right - below * right[j:j + 1]
        left, right = left * scale, right * scale
        d_ref[r0:r0 + G, :NB] = left
        d_ref[r0:r0 + G, NB:] = right
        if r0 + G < NB:
            both = jnp.concatenate([left, right], axis=1)
            h, m, l = split3(both)
            a = jnp.concatenate([v[:, :NB] for v in (h, h, m, m, h, l)], axis=0)
            b = jnp.concatenate([h, m, h, m, l, h], axis=0).astype(jnp.bfloat16)
            at = a.T.astype(jnp.bfloat16)
            upd = jnp.dot(at, b, preferred_element_type=jnp.float32)
            d_ref[r0 + G:, :] = d_ref[r0 + G:, :] - upd[r0 + G:, :]


def factor(m_ref, d_ref, size, between):
    eye = (lax.broadcasted_iota(jnp.int32, (NB, NB), 0) == lax.broadcasted_iota(jnp.int32, (NB, NB), 1)).astype(jnp.float32)
    steps = size // NB
    for k in range(steps):
        at, window = slice(k * NB, (k + 1) * NB), slice(k * NB, (k + 1) * NB + size)
        d_ref[:, :NB] = m_ref[at, at]
        d_ref[:, NB:] = eye
        factor_block(d_ref)
        done = dot3(split2(d_ref[:, NB:]), split2(m_ref[at, window]))
        m_ref[at, window] = done
        if k + 1 < steps:
            done = split2(done)
            right = tuple(v[:, NB:size - k * NB] for v in done)
            m_ref[(k + 1) * NB:, window] = m_ref[(k + 1) * NB:, window] - dot3(right, done, TN)
        between(k + 1)


def tiles(steps, split, col):
    if split == 1:
        return [(i, j) for i in range(steps) for j in range(i, steps)]
    first = [(col, col + t) for t in range(steps - col)]
    return first + [(steps - 1 - col, j) for j in range(steps - 1 - col, steps)]


class Sum:
    def __init__(self, n1, n2, part, got1, mid, got2, full, send, recv):
        self.n1, self.n2 = n1, n2
        self.part, self.got1, self.mid, self.got2, self.full = part, got1, mid, got2, full
        self.send, self.recv = send, recv
        me = lax.axis_index("row")
        self.outer, self.inner = me // n1, lax.rem(me, n1)
        self.col = lax.axis_index("col")

    def copies(self, phase):
        n1, n2, inner, outer = self.n1, self.n2, self.inner, self.outer
        first = (0, n1 - 1, n1 + n2 - 2, n1 + 2 * n2 - 3)[phase]
        out = []
        for k in range(1, n1 if phase in (0, 3) else n2):
            if phase in (0, 3):
                peer = lax.rem(inner + k, n1)
                target = outer * n1 + peer
            else:
                peer = lax.rem(outer + k, n2)
                target = peer * n1 + inner
            if phase == 0:
                src, dst = self.part.at[peer], self.got1.at[k - 1]
            elif phase == 1:
                src, dst = self.mid.at[peer], self.got2.at[k - 1]
            elif phase == 2:
                src = dst = self.full.at[inner, outer]
            else:
                src = dst = self.full.at[inner]
            out.append(pltpu.make_async_remote_copy(
                src_ref=src, dst_ref=dst, send_sem=self.send.at[first + k - 1],
                recv_sem=self.recv.at[first + k - 1], device_id=(target, self.col),
                device_id_type=pl.DeviceIdType.MESH))
        return out

    def start(self, phase):
        for copy in self.copies(phase):
            copy.start()

    def finish(self, phase):
        if phase == 0:
            total = self.part[self.inner]
            for k, copy in enumerate(self.copies(0)):
                copy.wait_recv()
                total = total + self.got1[k]
            self.mid[...] = total
        elif phase == 1:
            total = self.mid[self.outer]
            for k, copy in enumerate(self.copies(1)):
                copy.wait_recv()
                total = total + self.got2[k]
            self.full[self.inner, self.outer] = total
        else:
            for copy in self.copies(phase):
                copy.wait_recv()

    def drain(self):
        for phase in range(4):
            for copy in self.copies(phase):
                copy.wait_send()


def kernel(n, m, n1, split, total_rows, panel_ref, trailing_ref, r_ref, out_ref, block, strip, gpart, ggot1, gmid, ggot2, gfull,
           cpart, cgot1, cmid, cgot2, cfull, m_ref, d_ref, gsend, grecv, csend, crecv, bsend, brecv, esend, erecv):
    n2 = n // n1
    size = panel_ref.shape[1]
    own = panel_ref.shape[0]
    row, col = lax.axis_index("row"), lax.axis_index("col")
    outer, inner = row // n1, lax.rem(row, n1)
    MESH = pl.DeviceIdType.MESH
    here = pl.when(row >= 0)
    barrier = pltpu.get_barrier_semaphore()
    for k in range(1, m):
        pl.semaphore_signal(barrier, inc=1, device_id=(row, lax.rem(col + k, m)), device_id_type=MESH)
    for k in range(1, n1):
        pl.semaphore_signal(barrier, inc=1, device_id=(outer * n1 + lax.rem(inner + k, n1), col), device_id_type=MESH)
    for k in range(1, n2):
        pl.semaphore_signal(barrier, inc=1, device_id=(lax.rem(outer + k, n2) * n1 + inner, col), device_id_type=MESH)
    pl.semaphore_wait(barrier, m + n1 + n2 - 3)

    def spread(src, dst, send, recv):
        return [pltpu.make_async_remote_copy(
            src_ref=src, dst_ref=dst, send_sem=send.at[k - 1], recv_sem=recv.at[k - 1],
            device_id=(row, lax.rem(col + k, m)), device_id_type=MESH) for k in range(1, m)]

    gather = spread(panel_ref, block.at[col], bsend, brecv)
    here(lambda: [copy.start() for copy in gather] and None)
    block[col] = panel_ref[...]

    steps = size // NB
    count = len(tiles(steps, split, 0))
    m_ref[:, :size] = jnp.zeros((size, size), jnp.float32)
    r = lax.broadcasted_iota(jnp.int32, (size, size), 0)
    c = lax.broadcasted_iota(jnp.int32, (size, size), 1)
    m_ref[:, size:] = (r == c).astype(jnp.float32)

    def cut(x, i):
        return x[:, pl.ds(pl.multiple_of(i * NB, NB), NB)]

    strips = range(steps) if split == 1 else (col, steps - 1 - col)

    def gram(x):
        return dot3(split2(jnp.concatenate([cut(x, i) for i in strips], axis=1)), split2(x[...]), TN)

    strip[...] = gram(panel_ref)
    for k, copy in enumerate(gather):
        copy.wait_recv()
        strip[...] = strip[...] + gram(block.at[lax.rem(col + m - k - 1, m)])
    if split == 1:
        picked = [strip[i * NB:(i + 1) * NB, j * NB:(j + 1) * NB] for i, j in tiles(steps, 1, 0)]
    else:
        picked = []
        for t in range(count):
            low = t >= steps - col
            i, j = jnp.where(low, 1, 0), jnp.where(low, t - 1, col + t)
            picked.append(strip[pl.ds(pl.multiple_of(i * NB, NB), NB), pl.ds(pl.multiple_of(j * NB, NB), NB)])
    gpart[...] = jnp.concatenate(picked, axis=0).reshape(gpart.shape)
    gsum = Sum(n1, n2, gpart, ggot1, gmid, ggot2, gfull.at[col if split > 1 else 0], gsend, grecv)
    csum = Sum(n1, n2, cpart, cgot1, cmid, cgot2, cfull, csend, crecv)
    here(lambda: gsum.start(0))
    cross = jnp.zeros((size, trailing_ref.shape[1]), jnp.float32)
    for k in range(m):
        cross = cross + dot3(split2(block[k]), split2(trailing_ref[k * own:(k + 1) * own, :]), TN)
    cpart[...] = cross.reshape(cpart.shape)
    here(lambda: csum.start(0))
    for phase in range(4):
        @here
        def _():
            gsum.finish(phase)
            if phase < 3:
                gsum.start(phase + 1)
    share = spread(gsum.full, gsum.full, esend, erecv) if split > 1 else []
    for copy in share:
        copy.start()
    for copy in share:
        copy.wait_recv()
    for k in range(split):
        flat = gfull[k].reshape(count * NB, NB)
        for t, (i, j) in enumerate(tiles(steps, split, k)):
            m_ref[i * NB:(i + 1) * NB, j * NB:(j + 1) * NB] = flat[t * NB:(t + 1) * NB]

    def between(k):
        for phase in range(4):
            if k == (steps if phase == 3 else phase * steps // 4):
                @here
                def _():
                    csum.finish(phase)
                    if phase < 3:
                        csum.start(phase + 1)

    between(0)
    factor(m_ref, d_ref, size, between)
    r_ref[...] = jnp.where(c >= r, m_ref[:, :size] * (1.0 / math.sqrt(total_rows)), 0.0)
    w = split2(m_ref[:, size:])
    coupling = dot3(w, split2(cfull[...].reshape(size, cfull.shape[-1])))
    combined = split2(dot3(w, split2(coupling), TN))
    for k in range(m):
        at = slice(k * own, (k + 1) * own)
        out_ref[at, :] = trailing_ref[at, :] - dot3(split2(block[k]), combined)
    gsum.drain()
    csum.drain()
    for copy in gather + share:
        copy.wait_send()


def per_device(panel, trailing):
    n, m = lax.axis_size("row"), lax.axis_size("col")
    own, size = panel.shape
    width = trailing.shape[1]
    n1 = 4 if n % 4 == 0 else n
    n2 = n // n1
    steps = size // NB
    split = m if steps == 2 * m and (steps + 1) * NB % (8 * n) == 0 else 1
    count = len(tiles(steps, split, 0))
    f32 = jnp.float32

    def buffers(rows, cols, copies):
        s = rows // n
        lead = (copies,) if copies else ()
        return [pltpu.VMEM((n1, n2, s, cols), f32), pltpu.VMEM((max(n1 - 1, 1), n2, s, cols), f32),
                pltpu.VMEM((n2, s, cols), f32), pltpu.VMEM((max(n2 - 1, 1), s, cols), f32),
                pltpu.VMEM(lead + (n1, n2, s, cols), f32)]

    dma = pltpu.SemaphoreType.DMA
    hops = 2 * (n1 + n2 - 2)
    vmem = pl.BlockSpec(memory_space=pltpu.VMEM)
    return pl.pallas_call(
        functools.partial(kernel, n, m, n1, split, own * n * m),
        out_shape=(jax.ShapeDtypeStruct((size, size), f32), jax.ShapeDtypeStruct(trailing.shape, f32)),
        in_specs=[vmem] * 2,
        out_specs=[vmem] * 2,
        scratch_shapes=[pltpu.VMEM((m, own, size), f32), pltpu.VMEM((size if split == 1 else 2 * NB, size), f32)]
        + buffers(count * NB, NB, split) + buffers(size, width, 0)
        + [pltpu.VMEM((size, 2 * size), f32), pltpu.VMEM((NB, 2 * NB), f32)]
        + [dma((hops,))] * 4 + [dma((max(m - 1, 1),))] * 4,
        compiler_params=pltpu.CompilerParams(collective_id=0, has_side_effects=True, vmem_limit_bytes=56 << 20),
    )(panel, trailing)


def solution(mesh):
    return jax.shard_map(
        per_device, mesh=mesh, in_specs=(P(("row", "col"), None), P("row", "col")),
        out_specs=(P(), P("row", "col")), check_vma=False)
```
